32 devices in a mesh: ctx: 8 (over z, x), fsdp: 4 (over y, core).
Axes of the slice: x: 2, y: 2, z: 4, core: 2. Of those that a mesh axis runs over, the one named last changes fastest.
Arguments:
- tokens: bfloat16 [2, 4, 2048, 1024], P(None, 'fsdp', 'ctx'), may hold values from -6 to 6
- lengths: int32 [2, 4], P(None, 'fsdp'), may hold values from 512 to 2048, as said below
- w_query: bfloat16 [1024, 1024], P('fsdp'), may hold values from -0.1875 to 0.1875
- w_key: bfloat16 [1024, 1024], P('fsdp'), may hold values from -0.1875 to 0.1875
- w_value: bfloat16 [1024, 1024], P('fsdp'), may hold values from -0.1875 to 0.1875
- w_mixgate: bfloat16 [1024, 1024], P('fsdp'), may hold values from -0.1875 to 0.1875
- w_output: bfloat16 [1024, 1024], P('fsdp'), may hold values from -1.5 to 1.5
- w_ffgate: bfloat16 [1024, 2816], P('fsdp'), may hold values from -0.1875 to 0.1875
- w_ffup: bfloat16 [1024, 2816], P('fsdp'), may hold values from -0.1875 to 0.1875
- w_ffdown: bfloat16 [2816, 1024], P('fsdp'), may hold values from -0.21875 to 0.21875
- conv_weight: float32 [3, 4, 1024], replicated, may hold values from -3 to 3
- norm_first: float32 [1024], replicated, may hold values from 0.5 to 1.5
- norm_second: float32 [1024], replicated, may hold values from 0.5 to 1.5
- ridge_log: float32 [1024], replicated, may hold values from 0 to 2.3
- out_grad: bfloat16 [2, 4, 2048, 1024], P(None, 'fsdp', 'ctx'), may hold values from -6 to 6
Outputs:
- result: bfloat16 [2, 4, 2048, 1024], P(None, 'fsdp', 'ctx')
- input_grad: bfloat16 [2, 4, 2048, 1024], P(None, 'fsdp', 'ctx')
- query_grad: float32 [1024, 1024], P(None, ('ctx', 'fsdp'))
- key_grad: float32 [1024, 1024], P(None, ('ctx', 'fsdp'))
- value_grad: float32 [1024, 1024], P(None, ('ctx', 'fsdp'))
- mixgate_grad: float32 [1024, 1024], P(None, ('ctx', 'fsdp'))
- output_grad: float32 [1024, 1024], P(None, ('ctx', 'fsdp'))
- ffgate_grad: float32 [1024, 2816], P(None, ('ctx', 'fsdp'))
- ffup_grad: float32 [1024, 2816], P(None, ('ctx', 'fsdp'))
- ffdown_grad: float32 [2816, 1024], P(None, ('ctx', 'fsdp'))
- conv_grad: float32 [3, 4, 1024], P(None, None, ('ctx', 'fsdp'))
- first_gain_grad: float32 [1024], P(('ctx', 'fsdp'))
- second_gain_grad: float32 [1024], P(('ctx', 'fsdp'))
- ridge_grad: float32 [1024], P(('ctx', 'fsdp'))
The draws below stay inside these ranges and needn't reach their ends.
Inputs may be any that keep to these rules, and one draw needn't show every extreme that they name: `lengths`: in each micro-batch one sequence, drawn from the seed, has length exactly 2048.
All inputs are finite; a program needn't handle non-finite values.
Results may differ from the reference program's by a relative error of at most 0.025.
Values may be sent and summed in bfloat16 or wider, within the bound.
No kernel may reach another device: no remote copies, remote signals or barrier semaphores. Data moves between devices by JAX's collectives and lax.ppermute only.
A program may use at most 448 MiB of HBM per device.

```python
import jax
import jax.numpy as jnp
import numpy as np
from jax import lax

D = 1024
HEAD_COUNT = 8
HEAD_SIZE = 128
FF = 2816
C = 128
KW = 4
ITERS = 2
MB = 2
CPD = 2
L = 2048
SEQS = 4
N_CTX = 8


def draw_lengths(key, part):
    key = jax.random.fold_in(key, 11)
    first, second = jax.random.split(key)
    drawn = jax.random.randint(first, (MB, SEQS), L // 4, L + 1)
    chosen = jax.random.randint(second, (MB, 1), 0, SEQS)
    return jnp.where(jnp.arange(SEQS)[None, :] == chosen, L, drawn).astype(jnp.int32)


def draw_ridge_log(key, part):
    key = jax.random.fold_in(key, 23)
    spread = jax.random.uniform(key, (D,), jnp.float32, 0.0, 1.0)
    return (2.3 * spread).astype(jnp.float32)


def block_levels(key, shape, cuts, low, high):
    loudness = 1.0
    for position, shards_of in cuts:
        steps = jax.random.uniform(jax.random.fold_in(jax.random.fold_in(key, 6), position), (shards_of,), jnp.float32, low / len(cuts), high / len(cuts))
        loudness = loudness * jnp.repeat(jnp.exp(steps), shape[position] // shards_of).reshape((-1,) + (1,) * (len(shape) - 1 - position))
    return loudness


def bell_draw(own_key, dims, scale, limit, cuts=(), kind=jnp.bfloat16):
    gain = block_levels(own_key, dims, cuts, -0.22, 0.18) if cuts else 1.0
    values = jax.random.normal(own_key, dims, jnp.float32) * scale * gain
    return jnp.minimum(jnp.maximum(values, -limit), limit).astype(kind)


def setup_inputs(seed: int = 0) -> dict:
    key_of = jax.random.split(jax.random.key(seed), 16)
    return {
        "tokens": bell_draw(key_of[0], (MB, SEQS, L, D), 1.0, 6.0, ((1, 4), (2, 8))),
        "lengths": draw_lengths(jax.random.fold_in(key_of[15], 71), 0),
        "w_query": bell_draw(key_of[2], (D, D), D ** -0.5, 0.1875, ((0, 4),)),
        "w_key": bell_draw(key_of[3], (D, D), D ** -0.5, 0.1875, ((0, 4),)),
        "w_value": bell_draw(key_of[4], (D, D), D ** -0.5, 0.1875, ((0, 4),)),
        "w_mixgate": bell_draw(key_of[5], (D, D), D ** -0.5, 0.1875, ((0, 4),)),
        "w_output": bell_draw(key_of[6], (D, D), (D // 64) ** -0.5, 1.5, ((0, 4),)),
        "w_ffgate": bell_draw(key_of[7], (D, FF), D ** -0.5, 0.1875, ((0, 4),)),
        "w_ffup": bell_draw(key_of[8], (D, FF), D ** -0.5, 0.1875, ((0, 4),)),
        "w_ffdown": bell_draw(key_of[9], (FF, D), (FF // 4) ** -0.5, 0.21875, ((0, 4),)),
        "conv_weight": bell_draw(key_of[10], (3, KW, D), 0.5, 3.0, (), jnp.float32),
        "norm_first": jnp.clip(1.0 + 0.1 * jax.random.normal(key_of[11], (D,), jnp.float32), 0.5, 1.5),
        "norm_second": jnp.clip(1.0 + 0.1 * jax.random.normal(key_of[12], (D,), jnp.float32), 0.5, 1.5),
        "ridge_log": draw_ridge_log(jax.random.fold_in(key_of[15], 71), 0),
        "out_grad": bell_draw(key_of[14], (MB, SEQS, L, D), 1.0, 6.0, ((1, 4), (2, 8))),
    }


EPS = 1e-06
HIGH = lax.Precision.HIGHEST

@jax.custom_vjp
def low(v):
    return lax.optimization_barrier(v.astype(jnp.bfloat16)).astype(jnp.float32)

@jax.custom_vjp
def low_back(v):
    return v

def low_keep(v):
    return (low(v), None)

def low_pass(kept, grad):
    return (grad,)

def back_keep(v):
    return (v, None)

def back_low(kept, grad):
    return (low(grad),)
low.defvjp(low_keep, low_pass)
low_back.defvjp(back_keep, back_low)

def sigmoid_linear(value):
    return value * jax.nn.sigmoid(value)

def mesa_block(queries, keys, values, ridge, state_kk, state_kv, valid):
    span = queries.shape[1]
    causal = jnp.tril(jnp.ones((span, span), queries.dtype))

    def apply_system(direc):
        inner = jnp.einsum('hcd,hed->hce', direc, keys, precision=HIGH) * causal
        image = jnp.einsum('hcd,hde->hce', direc, state_kk, precision=HIGH)
        image = image + jnp.einsum('hce,hed->hcd', inner, keys, precision=HIGH)
        return image + ridge[:, None, :] * direc
    solution = jnp.zeros_like(queries)
    residue = queries
    direc = queries
    squares = lax.optimization_barrier(jnp.sum(residue * residue, -1, keepdims=True))
    for step in range(ITERS):
        image = apply_system(direc)
        alpha = squares / lax.optimization_barrier(jnp.sum(direc * image, -1, keepdims=True))
        solution = solution + alpha * direc
        residue = residue - alpha * image
        if step + 1 < ITERS:
            fresh = lax.optimization_barrier(jnp.sum(residue * residue, -1, keepdims=True))
            direc = residue + fresh / squares * direc
            squares = fresh
    inner = jnp.einsum('hcd,hed->hce', solution, keys, precision=HIGH) * causal
    mixed = jnp.einsum('hcd,hde->hce', solution, state_kv, precision=HIGH)
    mixed = mixed + jnp.einsum('hce,hed->hcd', inner, values, precision=HIGH)
    return mixed * valid[None, :, None]

def product(left, right):
    return jnp.dot(left, right, precision=HIGH, preferred_element_type=jnp.float32)

def rms_scale(rows):
    return lax.rsqrt(lax.optimization_barrier(jnp.mean(rows * rows, -1, keepdims=True)) + EPS)

def unit_heads(rows):
    return rows * lax.rsqrt(lax.optimization_barrier(jnp.sum(rows * rows, -1, keepdims=True)) + EPS)

def sequence(inputs, valid, params):
    w_query, w_key, w_value, w_mixgate, w_output, w_ffgate, w_ffup, w_ffdown, conv_weight, norm_first, norm_second, ridge_log = params
    total = inputs.shape[0]
    width = inputs.shape[1]
    normed = low(inputs * rms_scale(inputs) * norm_first)
    pre_query = low_back(product(normed, w_query))
    pre_key = low_back(product(normed, w_key))
    pre_value = low_back(product(normed, w_value))
    pre_gate = low_back(product(normed, w_mixgate))
    joined = jnp.concatenate([pre_query, pre_key, pre_value], -1)
    kernel = conv_weight.shape[1]
    taps = jnp.transpose(conv_weight, (1, 0, 2)).reshape(kernel, 3 * width)
    padded = jnp.concatenate([jnp.zeros((kernel - 1, 3 * width), inputs.dtype), joined], 0)
    convolved = taps[0] * joined
    for lag in range(1, kernel):
        convolved = convolved + taps[lag] * padded[kernel - 1 - lag:kernel - 1 - lag + total]
    activated = sigmoid_linear(convolved)

    def heads(rows):
        return rows.reshape(total // C, C, HEAD_COUNT, HEAD_SIZE).transpose(0, 2, 1, 3)
    valid_blocks = valid.reshape(total // C, C)
    mask = valid_blocks[:, None, :, None]
    queries = unit_heads(heads(activated[:, :width]))
    keys = unit_heads(heads(activated[:, width:2 * width])) * mask
    values = heads(activated[:, 2 * width:]) * mask
    ridge = jnp.exp(ridge_log).reshape(HEAD_COUNT, HEAD_SIZE)
    solve_block = jax.checkpoint(mesa_block)

    def advance(carry, pieces):
        state_kk, state_kv = carry
        block_queries, block_keys, block_values, block_valid = pieces
        mixed = solve_block(block_queries, block_keys, block_values, ridge, state_kk, state_kv, block_valid)
        state_kk = state_kk + jnp.einsum('hcd,hce->hde', block_keys, block_keys, precision=HIGH)
        state_kv = state_kv + jnp.einsum('hcd,hce->hde', block_keys, block_values, precision=HIGH)
        return ((state_kk, state_kv), mixed)
    zero_state = jnp.zeros((HEAD_COUNT, HEAD_SIZE, HEAD_SIZE), inputs.dtype)
    _, mixed = lax.scan(advance, (zero_state, zero_state), (queries, keys, values, valid_blocks))
    mixed_rows = mixed.transpose(0, 2, 1, 3).reshape(total, width)
    gated = low(mixed_rows * sigmoid_linear(pre_gate))
    middle = inputs + low_back(product(gated, w_output))
    normed_two = low(middle * rms_scale(middle) * norm_second)
    swish_pre = low_back(product(normed_two, w_ffgate))
    lift = low_back(product(normed_two, w_ffup))
    hidden = low(sigmoid_linear(swish_pre) * lift)
    return middle + low_back(product(hidden, w_ffdown))

def dealt_positions():
    slots = np.arange(L)
    device = slots // (CPD * C)
    within = slots // C % CPD
    pair = within // 2
    number = pair * 2 * N_CTX + np.where(within % 2 == 0, device, 2 * N_CTX - 1 - device)
    return number * C + slots % C

def reference(tokens, lengths, w_query, w_key, w_value, w_mixgate, w_output, w_ffgate, w_ffup, w_ffdown, conv_weight, norm_first, norm_second, ridge_log, out_grad):
    order = dealt_positions()
    back = np.argsort(order)
    natural = tokens.astype(jnp.float32)[:, :, back, :]
    cotangent = out_grad.astype(jnp.float32)[:, :, back, :]
    valid = (jnp.arange(L, dtype=jnp.int32)[None, None, :] < lengths[:, :, None]).astype(jnp.float32)
    params = tuple((w.astype(jnp.float32) for w in (w_query, w_key, w_value, w_mixgate, w_output, w_ffgate, w_ffup, w_ffdown)))
    params = params + (conv_weight, norm_first, norm_second, ridge_log)
    run = jax.checkpoint(sequence)

    def forward(inputs, weights):
        flat = inputs.reshape(MB * SEQS, L, D)
        flat_valid = valid.reshape(MB * SEQS, L).astype(inputs.dtype)
        outputs = lax.map(lambda pieces: run(pieces[0], pieces[1], weights), (flat, flat_valid))
        return outputs.reshape(inputs.shape)
    result, pullback_function = jax.vjp(forward, natural, params)
    grad_inputs, grads = pullback_function(cotangent)
    result = result[:, :, order, :].astype(jnp.bfloat16)
    grad_inputs = grad_inputs[:, :, order, :].astype(jnp.bfloat16)
    return (result, grad_inputs, grads[0], grads[1], grads[2], grads[3], grads[4], grads[5], grads[6], grads[7], grads[8], grads[9], grads[10], grads[11])
```

```python
from functools import partial

import jax
import jax.numpy as jnp
from jax import lax
from jax.experimental import pallas as pl
from jax.experimental.pallas import tpu as pltpu
from jax.sharding import PartitionSpec as P

HEAD_COUNT = 8
HEAD_SIZE = 128
C = 128
EPS = 1e-06
GROUP = 4
PAD = 8
BF = jnp.bfloat16
F32 = jnp.float32
VMEM_BYTES = 56 * 1024 * 1024


def nn(a, b):
    return lax.dot_general(a, b, (((1,), (0,)), ((), ())), preferred_element_type=F32)


def nt(a, b):
    return lax.dot_general(a, b, (((1,), (1,)), ((), ())), preferred_element_type=F32)


def tn(a, b):
    return lax.dot_general(a, b, (((0,), (0,)), ((), ())), preferred_element_type=F32)


def silu(v):
    return v * jax.nn.sigmoid(v)


def slope(v):
    s = jax.nn.sigmoid(v)
    return s * (1.0 + v * (1.0 - s))


def rowsum(v):
    return jnp.sum(v, -1, keepdims=True)


def place_of(step, count):
    per_half = count // GROUP
    pair = step // (2 * per_half)
    rest = step % (2 * per_half)
    first = rest < per_half
    group = jnp.where(first, rest, 2 * per_half - 1 - rest)
    return group, pair * 2 + jnp.where(first, 0, 1), first


def causal_mask():
    rows = lax.broadcasted_iota(jnp.int32, (C, C), 0)
    cols = lax.broadcasted_iota(jnp.int32, (C, C), 1)
    return rows >= cols


def valid_rows(step, length):
    pos = step * (GROUP * C) + lax.broadcasted_iota(jnp.int32, (GROUP * C, 1), 0)
    return (pos < length).astype(F32)


def solve(q, k, kb, skk, ridge, tri):
    system = jnp.concatenate([kb, skk], 0)
    qb = q.astype(BF)
    inner0 = jnp.where(tri, nt(qb, kb), 0.0)
    i0 = nn(jnp.concatenate([inner0.astype(BF), qb], 1), system) + ridge * q
    rr0 = rowsum(q * q)
    p0 = rowsum(q * i0)
    a0 = rr0 / p0
    r1 = q - a0 * i0
    f = rowsum(r1 * r1)
    b = f / rr0
    d1 = r1 + b * q
    db = d1.astype(BF)
    inner1 = jnp.where(tri, nt(db, kb), 0.0)
    i1 = nn(jnp.concatenate([inner1.astype(BF), db], 1), system) + ridge * d1
    p1 = rowsum(d1 * i1)
    a1 = f / p1
    s2 = a0 * q + a1 * d1
    return system, qb, inner0, i0, rr0, p0, a0, r1, f, b, d1, inner1, i1, p1, a1, s2


def forward_kernel(
    count, len_ref, x_ref, w_ref, taps_ref, ridge_ref,
    gated_ref, pre_ref, mixed_ref, states_ref,
    padded, q_s, k_s, v_s, skk, skv,
):
    micro, step = pl.program_id(0), pl.program_id(1)
    _, _, first = place_of(step, count)
    span = GROUP * C

    @pl.when(step == 0)
    def _():
        padded[0:PAD, :] = jnp.zeros((PAD, 3 * HEAD_SIZE), F32)
        skk[...] = jnp.zeros_like(skk)
        skv[...] = jnp.zeros_like(skv)

    pre = nn(x_ref[...].reshape(span, x_ref.shape[-1]), w_ref[...])
    pre_ref[...] = pre.reshape(pre_ref.shape)
    for j in range(GROUP):
        jj = jnp.where(first, j, GROUP - 1 - j)
        padded[PAD + j * C : PAD + (j + 1) * C, :] = pre_ref[jj, 0, 0, :, : 3 * HEAD_SIZE]
    conv = taps_ref[0:1, :] * padded[PAD : PAD + span, :]
    for lag in range(1, 4):
        conv = conv + taps_ref[lag : lag + 1, :] * padded[PAD - lag : PAD - lag + span, :]
    padded[0:PAD, :] = padded[span : span + PAD, :]
    act = silu(conv)
    valid = valid_rows(step, len_ref[micro])
    act_q = act[:, :HEAD_SIZE]
    act_k = act[:, HEAD_SIZE : 2 * HEAD_SIZE]
    q_s[...] = act_q * lax.rsqrt(rowsum(act_q * act_q) + EPS)
    k_s[...] = act_k * (lax.rsqrt(rowsum(act_k * act_k) + EPS) * valid)
    v_s[...] = act[:, 2 * HEAD_SIZE :] * valid
    tri = causal_mask()
    ridge = ridge_ref[...]
    for j in range(GROUP):
        jj = jnp.where(first, j, GROUP - 1 - j)
        rows = slice(j * C, (j + 1) * C)
        k = k_s[rows, :]
        kb = k.astype(BF)
        vb = v_s[rows, :].astype(BF)
        kk_now = skk[...]
        kv_now = skv[...]
        states_ref[jj, 0, 0, 0] = kk_now
        states_ref[jj, 0, 0, 1] = kv_now
        s2 = solve(q_s[rows, :], k, kb, kk_now.astype(BF), ridge, tri)[-1]
        sb = s2.astype(BF)
        p = jnp.where(tri, nt(sb, kb), 0.0)
        mixed = nn(
            jnp.concatenate([p.astype(BF), sb], 1),
            jnp.concatenate([vb, kv_now.astype(BF)], 0),
        )
        mixed = mixed * valid[rows, :]
        mixed_ref[jj, 0, 0] = mixed
        gate = pre_ref[jj, 0, 0, :, 3 * HEAD_SIZE :]
        gated_ref[jj, 0, 0] = (mixed * silu(gate)).astype(BF)
        skk[...] = kk_now + tn(kb, kb)
        skv[...] = kv_now + tn(kb, vb)


def attention_forward(lengths, x, w, taps, ridge):
    count, micros, slots = x.shape[:3]
    width = x.shape[-1]
    steps = count * slots // GROUP

    def at(m, s):
        group, slot, _ = place_of(s, count)
        return (group, m, slot, 0, 0)

    def at_state(m, s):
        group, slot, _ = place_of(s, count)
        return (group, m, slot, 0, 0, 0)

    def block(columns):
        return pl.BlockSpec((GROUP, 1, 1, C, columns), at)

    whole = lambda shape: pl.BlockSpec(shape, lambda m, s: (0,) * len(shape))
    lead = (count, micros, slots, C)
    return pl.pallas_call(
        partial(forward_kernel, count),
        grid=(micros, steps),
        in_specs=[
            pl.BlockSpec(memory_space=pltpu.SMEM),
            block(width),
            whole(w.shape),
            whole(taps.shape),
            whole(ridge.shape),
        ],
        out_specs=[
            block(HEAD_SIZE),
            block(4 * HEAD_SIZE),
            block(HEAD_SIZE),
            pl.BlockSpec((GROUP, 1, 1, 2, HEAD_SIZE, HEAD_SIZE), at_state),
        ],
        out_shape=[
            jax.ShapeDtypeStruct((*lead, HEAD_SIZE), BF),
            jax.ShapeDtypeStruct((*lead, 4 * HEAD_SIZE), F32),
            jax.ShapeDtypeStruct((*lead, HEAD_SIZE), F32),
            jax.ShapeDtypeStruct((count, micros, slots, 2, HEAD_SIZE, HEAD_SIZE), F32),
        ],
        scratch_shapes=[
            pltpu.VMEM((GROUP * C + PAD, 3 * HEAD_SIZE), F32),
            pltpu.VMEM((GROUP * C, HEAD_SIZE), F32),
            pltpu.VMEM((GROUP * C, HEAD_SIZE), F32),
            pltpu.VMEM((GROUP * C, HEAD_SIZE), F32),
            pltpu.VMEM((HEAD_SIZE, HEAD_SIZE), F32),
            pltpu.VMEM((HEAD_SIZE, HEAD_SIZE), F32),
        ],
        compiler_params=pltpu.CompilerParams(vmem_limit_bytes=VMEM_BYTES),
        cost_estimate=pl.CostEstimate(
            flops=2 * count * micros * slots * C * (width * 512 + 11 * C * C),
            bytes_accessed=count * micros * slots * C * (2 * width + 4096),
            transcendentals=0,
        ),
        name="attn_forward",
    )(lengths, x, w, taps, ridge)


def backward_kernel(
    count, steps, len_ref, x_ref, g_ref, pre_ref, tail_ref, mixed_ref, states_ref, taps_ref, ridge_ref,
    dpre_ref, dw_ref, dtaps_ref, dridge_ref,
    padded, conv_s, act_s, q_s, k_s, dq_s, dk_s, dv_s, ext, gsum, hsum,
):
    micro, turn = pl.program_id(0), pl.program_id(1)
    step = steps - 1 - turn
    _, _, first = place_of(step, count)
    span = GROUP * C

    @pl.when(turn == 0)
    def _():
        ext[span : span + PAD, :] = jnp.zeros((PAD, 3 * HEAD_SIZE), F32)
        gsum[...] = jnp.zeros_like(gsum)
        hsum[...] = jnp.zeros_like(hsum)

    @pl.when((turn == 0) & (micro == 0))
    def _():
        dw_ref[...] = jnp.zeros_like(dw_ref)
        dtaps_ref[...] = jnp.zeros_like(dtaps_ref)
        dridge_ref[...] = jnp.zeros_like(dridge_ref)

    keep = jnp.where(step > 0, 1.0, 0.0)
    padded[0:PAD, :] = tail_ref[0, 0, 0, :, : 3 * HEAD_SIZE] * keep
    for j in range(GROUP):
        jj = jnp.where(first, j, GROUP - 1 - j)
        padded[PAD + j * C : PAD + (j + 1) * C, :] = pre_ref[jj, 0, 0, :, : 3 * HEAD_SIZE]
    conv = taps_ref[0:1, :] * padded[PAD : PAD + span, :]
    for lag in range(1, 4):
        conv = conv + taps_ref[lag : lag + 1, :] * padded[PAD - lag : PAD - lag + span, :]
    conv_s[...] = conv
    act = silu(conv)
    act_s[...] = act
    valid = valid_rows(step, len_ref[micro])
    act_q = act[:, :HEAD_SIZE]
    act_k = act[:, HEAD_SIZE : 2 * HEAD_SIZE]
    scale_q = lax.rsqrt(rowsum(act_q * act_q) + EPS)
    scale_k = lax.rsqrt(rowsum(act_k * act_k) + EPS)
    q_s[...] = act_q * scale_q
    k_s[...] = act_k * (scale_k * valid)
    tri = causal_mask()
    ridge = ridge_ref[...]
    ridge_total = jnp.zeros((1, HEAD_SIZE), F32)
    for j in reversed(range(GROUP)):
        jj = jnp.where(first, j, GROUP - 1 - j)
        rows = slice(j * C, (j + 1) * C)
        q = q_s[rows, :]
        k = k_s[rows, :]
        kb = k.astype(BF)
        vb = (act_s[rows, 2 * HEAD_SIZE :] * valid[rows, :]).astype(BF)
        skk = states_ref[jj, 0, 0, 0].astype(BF)
        skv = states_ref[jj, 0, 0, 1].astype(BF)
        system, qb, inner0, i0, rr0, p0, a0, r1, f, b, d1, inner1, i1, p1, a1, s2 = solve(
            q, k, kb, skk, ridge, tri
        )
        gate = pre_ref[jj, 0, 0, :, 3 * HEAD_SIZE :]
        d_gated = g_ref[jj, 0, 0].astype(F32)
        dpre_ref[jj, 0, 0, :, 3 * HEAD_SIZE :] = (
            d_gated * mixed_ref[jj, 0, 0] * slope(gate)
        ).astype(BF)
        g = (d_gated * silu(gate) * valid[rows, :]).astype(BF)
        sb = s2.astype(BF)
        p = jnp.where(tri, nt(sb, kb), 0.0)
        back = jnp.where(tri, nt(g, vb), 0.0)
        backb = back.astype(BF)
        ds = nn(backb, kb) + nt(g, skv)
        da1 = rowsum(ds * d1)
        df = da1 / p1
        dp1 = -df * a1
        dd1 = a1 * ds + (2.0 * dp1) * i1
        dbeta = rowsum(dd1 * q)
        inv_rr = 1.0 / rr0
        df = df + dbeta * inv_rr
        drr = -dbeta * b * inv_rr
        dr1 = dd1 + (2.0 * df) * r1
        da0 = rowsum(ds * q - dr1 * i0)
        da0p = da0 / p0
        drr = drr + da0p
        dp0 = -da0p * a0
        drb = dr1.astype(BF)
        innerr = jnp.where(tri, nt(drb, kb), 0.0)
        adr = nn(jnp.concatenate([innerr.astype(BF), drb], 1), system) + ridge * dr1
        dd0 = b * dd1 + a0 * ds + (2.0 * dp0) * i0 - a0 * adr
        di0 = dp0 * q - a0 * dr1
        dq_s[rows, :] = dr1 + dd0 + (2.0 * drr) * q
        wd1 = (2.0 * dp1) * d1
        ridge_total = ridge_total + jnp.sum(0.5 * wd1 * d1 + di0 * q, 0, keepdims=True)
        inneri = dp0 * inner0 - a0 * innerr
        di0b = di0.astype(BF)
        d1b = d1.astype(BF)
        wd1b = wd1.astype(BF)
        left = jnp.concatenate(
            [backb, inner1.astype(BF), inner0.astype(BF), inneri.astype(BF)], 0
        )
        right = jnp.concatenate([sb, wd1b, di0b, qb], 0)
        g_now = gsum[...]
        h_now = hsum[...]
        hb = h_now.astype(BF)
        dk_s[rows, :] = tn(left, right) + nn(kb, g_now.astype(BF)) + nt(vb, hb)
        both = tn(jnp.concatenate([p.astype(BF), sb], 1), g)
        dv_s[rows, :] = both[:C] + nn(kb, hb)
        hsum[...] = h_now + both[C:]
        gsum[...] = g_now + tn(
            jnp.concatenate([d1b, di0b, qb], 0), jnp.concatenate([wd1b, qb, di0b], 0)
        )
    dridge_ref[...] += ridge_total
    act = act_s[...]
    act_q = act[:, :HEAD_SIZE]
    act_k = act[:, HEAD_SIZE : 2 * HEAD_SIZE]
    dq = dq_s[...]
    dk = dk_s[...] * valid
    d_act_q = scale_q * dq - act_q * (scale_q * scale_q * scale_q * rowsum(dq * act_q))
    d_act_k = scale_k * dk - act_k * (scale_k * scale_k * scale_k * rowsum(dk * act_k))
    d_act = jnp.concatenate([d_act_q, d_act_k, dv_s[...] * valid], 1)
    ext[0:span, :] = d_act * slope(conv_s[...])
    now = padded[PAD : PAD + span, :]
    shifted = ext[0:span, :]
    d_pre = taps_ref[0:1, :] * shifted
    dtaps_ref[0:1, :] += jnp.sum(shifted * now, 0, keepdims=True)
    for lag in range(1, 4):
        shifted = ext[lag : lag + span, :]
        d_pre = d_pre + taps_ref[lag : lag + 1, :] * shifted
        dtaps_ref[lag : lag + 1, :] += jnp.sum(shifted * now, 0, keepdims=True)
    ext[span : span + PAD, :] = ext[0:PAD, :]
    d_pre = d_pre.astype(BF)
    for j in range(GROUP):
        jj = jnp.where(first, j, GROUP - 1 - j)
        dpre_ref[jj, 0, 0, :, : 3 * HEAD_SIZE] = d_pre[j * C : (j + 1) * C, :]
    dw_ref[...] += tn(
        dpre_ref[...].reshape(span, 4 * HEAD_SIZE), x_ref[...].reshape(span, x_ref.shape[-1])
    )


def attention_backward(lengths, x, d_gated, pre, mixed, states, taps, ridge):
    count, micros, slots = x.shape[:3]
    width = x.shape[-1]
    steps = count * slots // GROUP

    def at(m, s):
        group, slot, _ = place_of(steps - 1 - s, count)
        return (group, m, slot, 0, 0)

    def at_state(m, s):
        group, slot, _ = place_of(steps - 1 - s, count)
        return (group, m, slot, 0, 0, 0)

    def at_tail(m, s):
        step = jnp.maximum(steps - 2 - s, 0)
        group, slot, first = place_of(step, count)
        device = group * GROUP + jnp.where(first, GROUP - 1, 0)
        return (device, m, slot, C // PAD - 1, 0)

    def block(columns):
        return pl.BlockSpec((GROUP, 1, 1, C, columns), at)

    whole = lambda shape: pl.BlockSpec(shape, lambda m, s: (0,) * len(shape))
    rows = GROUP * C
    return pl.pallas_call(
        partial(backward_kernel, count, steps),
        grid=(micros, steps),
        in_specs=[
            pl.BlockSpec(memory_space=pltpu.SMEM),
            block(width),
            block(HEAD_SIZE),
            block(4 * HEAD_SIZE),
            pl.BlockSpec((1, 1, 1, PAD, 4 * HEAD_SIZE), at_tail),
            block(HEAD_SIZE),
            pl.BlockSpec((GROUP, 1, 1, 2, HEAD_SIZE, HEAD_SIZE), at_state),
            whole(taps.shape),
            whole(ridge.shape),
        ],
        out_specs=[
            block(4 * HEAD_SIZE),
            whole((4 * HEAD_SIZE, width)),
            whole((PAD, 3 * HEAD_SIZE)),
            whole((1, HEAD_SIZE)),
        ],
        out_shape=[
            jax.ShapeDtypeStruct((count, micros, slots, C, 4 * HEAD_SIZE), BF),
            jax.ShapeDtypeStruct((4 * HEAD_SIZE, width), F32),
            jax.ShapeDtypeStruct((PAD, 3 * HEAD_SIZE), F32),
            jax.ShapeDtypeStruct((1, HEAD_SIZE), F32),
        ],
        scratch_shapes=[
            pltpu.VMEM((rows + PAD, 3 * HEAD_SIZE), F32),
            pltpu.VMEM((rows, 3 * HEAD_SIZE), F32),
            pltpu.VMEM((rows, 3 * HEAD_SIZE), F32),
            pltpu.VMEM((rows, HEAD_SIZE), F32),
            pltpu.VMEM((rows, HEAD_SIZE), F32),
            pltpu.VMEM((rows, HEAD_SIZE), F32),
            pltpu.VMEM((rows, HEAD_SIZE), F32),
            pltpu.VMEM((rows, HEAD_SIZE), F32),
            pltpu.VMEM((rows + PAD, 3 * HEAD_SIZE), F32),
            pltpu.VMEM((HEAD_SIZE, HEAD_SIZE), F32),
            pltpu.VMEM((HEAD_SIZE, HEAD_SIZE), F32),
        ],
        compiler_params=pltpu.CompilerParams(vmem_limit_bytes=VMEM_BYTES),
        cost_estimate=pl.CostEstimate(
            flops=2 * count * micros * slots * C * (width * 512 + 24 * C * C),
            bytes_accessed=count * micros * slots * C * (2 * width + 4096),
            transcendentals=0,
        ),
        name="attn_backward",
    )(lengths, x, d_gated, pre, pre, mixed, states, taps, ridge)


def ff_kernel(
    x_ref, up_ref, mid_ref, wg_ref, wu_ref, wd_ref,
    res_ref, d2_ref, gg_ref, gu_ref, gd_ref, total,
):
    tile = pl.program_id(0)
    last = pl.num_programs(0) - 1

    @pl.when(tile == 0)
    def _():
        total[...] = mid_ref[...]
        d2_ref[...] = jnp.zeros_like(d2_ref)

    x = x_ref[...]
    up = up_ref[...]
    swish_pre = nn(x, wg_ref[...])
    lift = nn(x, wu_ref[...])
    sig = jax.nn.sigmoid(swish_pre)
    swish = swish_pre * sig
    hidden = (swish * lift).astype(BF)
    total[...] += nn(hidden, wd_ref[...])
    d_hidden = nt(up, wd_ref[...])
    d_swish = (d_hidden * lift * (sig * (1.0 + swish_pre * (1.0 - sig)))).astype(BF)
    d_lift = (d_hidden * swish).astype(BF)
    d2_ref[...] += nt(d_swish, wg_ref[...]) + nt(d_lift, wu_ref[...])
    gg_ref[...] = tn(d_swish, x).astype(BF)
    gu_ref[...] = tn(d_lift, x).astype(BF)
    gd_ref[...] = tn(up, hidden).astype(BF)

    @pl.when(tile == last)
    def _():
        res_ref[...] = total[...].astype(BF)


def feed_forward(x, up, middle, wg, wu, wd):
    rows, width = x.shape
    ff = wg.shape[1]
    tile = 256
    whole = pl.BlockSpec((rows, width), lambda t: (0, 0))
    across = pl.BlockSpec((width, tile), lambda t: (0, t))
    down = pl.BlockSpec((tile, width), lambda t: (t, 0))
    return pl.pallas_call(
        ff_kernel,
        grid=(ff // tile,),
        in_specs=[whole, whole, whole, across, across, down],
        out_specs=[whole, whole, down, down, across],
        out_shape=[
            jax.ShapeDtypeStruct((rows, width), BF),
            jax.ShapeDtypeStruct((rows, width), F32),
            jax.ShapeDtypeStruct((ff, width), BF),
            jax.ShapeDtypeStruct((ff, width), BF),
            jax.ShapeDtypeStruct((width, ff), BF),
        ],
        scratch_shapes=[pltpu.VMEM((rows, width), F32)],
        compiler_params=pltpu.CompilerParams(vmem_limit_bytes=VMEM_BYTES),
        cost_estimate=pl.CostEstimate(
            flops=18 * rows * width * ff, bytes_accessed=12 * width * ff, transcendentals=rows * ff
        ),
        name="feed_forward",
    )(x, up, middle, wg, wu, wd)


def body(
    tokens,
    lengths,
    w_query,
    w_key,
    w_value,
    w_mixgate,
    w_output,
    w_ffgate,
    w_ffup,
    w_ffdown,
    conv_weight,
    norm_first,
    norm_second,
    ridge_log,
    out_grad,
):
    micros, _, rows, width = tokens.shape
    taps_count = conv_weight.shape[1]
    count = lax.axis_size("ctx")
    shards = lax.axis_size("fsdp")
    place = lax.axis_index("ctx")
    share = count // HEAD_COUNT
    own = max(micros // share, 1)
    copies = share * own // micros
    head = place // share
    column = head * HEAD_SIZE
    slots = rows // C
    every = micros * rows
    both = ("ctx", "fsdp")

    def gathered(w):
        return lax.all_gather(w, "fsdp", axis=0, tiled=True)

    def of_head(w, axis):
        return lax.dynamic_slice_in_dim(w, column, HEAD_SIZE, axis)

    inputs = tokens.reshape(every, width).astype(F32)
    first_scale = lax.rsqrt(jnp.mean(inputs * inputs, -1, keepdims=True) + EPS)
    normed = (inputs * first_scale * norm_first).astype(BF)
    x = lax.all_gather(normed.reshape(micros, rows, width), "ctx", axis=0)
    mine = lax.rem(place, share) // copies * own
    if share > 1:
        x = lax.dynamic_slice_in_dim(x, mine, own, 1)
    x = x.reshape(count, own, slots, C, width)
    own_lengths = lax.dynamic_slice_in_dim(lengths[:, 0], mine, own, 0)
    projections = (w_query, w_key, w_value, w_mixgate)
    w_head = gathered(jnp.concatenate([of_head(w, 1) for w in projections], 1))
    taps = of_head(conv_weight, 2).transpose(1, 0, 2).reshape(taps_count, 3 * HEAD_SIZE)
    ridge = jnp.exp(of_head(ridge_log, 0))[None]
    gated_head, pre, mixed, states = attention_forward(own_lengths, x, w_head, taps, ridge)

    def to_rows(value):
        columns = value.shape[-1]
        value = lax.all_to_all(value.reshape(count, own, rows, columns), "ctx", 0, 0)
        value = value.reshape(HEAD_COUNT, share // copies, copies, own, rows, columns)[:, :, 0]
        value = value.reshape(HEAD_COUNT, micros, rows, columns)
        return value.transpose(1, 2, 0, 3).reshape(every, HEAD_COUNT, columns)

    def to_heads(value):
        value = value.reshape(micros, rows, HEAD_COUNT, HEAD_SIZE).transpose(2, 0, 1, 3)
        value = value.reshape(HEAD_COUNT, share // copies, 1, own, rows, HEAD_SIZE)
        value = jnp.broadcast_to(value, (*value.shape[:2], copies, *value.shape[3:]))
        value = lax.all_to_all(value.reshape(count, own, rows, HEAD_SIZE), "ctx", 0, 0)
        return value.reshape(count, own, slots, C, HEAD_SIZE)

    full_output = gathered(w_output)
    full_ffgate = gathered(w_ffgate)
    full_ffup = gathered(w_ffup)
    full_ffdown = gathered(w_ffdown)
    gated = to_rows(gated_head).reshape(every, width)
    middle = inputs + nn(gated, full_output)
    second_scale = lax.rsqrt(jnp.mean(middle * middle, -1, keepdims=True) + EPS)
    normed_two = (middle * second_scale * norm_second).astype(BF)
    upstream = out_grad.reshape(every, width)
    result, grad_two, gate_t, up_t, down_t = feed_forward(
        normed_two, upstream, middle, full_ffgate, full_ffup, full_ffdown
    )
    scaled_two = grad_two * norm_second
    gain_second = jnp.sum(grad_two * middle * second_scale, 0)
    grad_middle = (
        second_scale * scaled_two
        - middle * second_scale**3 * jnp.mean(scaled_two * middle, -1, keepdims=True)
        + upstream.astype(F32)
    )
    grad_branch = grad_middle.astype(BF)
    output_t = tn(grad_branch, gated).astype(BF)
    grad_gated = nt(grad_branch, full_output).astype(BF)
    d_pre, dw, dtaps, dridge = attention_backward(
        own_lengths, x, to_heads(grad_gated), pre, mixed, states, taps, ridge
    )

    def scattered(value):
        return lax.psum_scatter(value, both, scatter_dimension=0, tiled=True).astype(F32).T

    grad_ffgate = scattered(gate_t)
    grad_ffup = scattered(up_t)
    grad_ffdown = scattered(down_t)
    grad_output = scattered(output_t)

    piece = HEAD_SIZE // share // shards
    dw = dw.reshape(4, share, shards, piece, width).transpose(1, 2, 0, 3, 4).astype(BF)
    small = jnp.concatenate(
        [
            dtaps[:taps_count].reshape(taps_count, 3, HEAD_SIZE).transpose(1, 0, 2).reshape(3 * taps_count, HEAD_SIZE),
            dridge * ridge,
        ],
        0,
    )
    small = small.reshape(-1, share, shards, piece).transpose(1, 2, 0, 3)
    if share > 1:
        groups = [[h * share + i for i in range(share)] for h in range(HEAD_COUNT)]
        counts = lax.rem(place, copies) == 0
        dw = jnp.where(counts, dw, jnp.zeros_like(dw))
        small = jnp.where(counts, small, 0.0)
        dw = lax.psum_scatter(dw, "ctx", scatter_dimension=0, axis_index_groups=groups)
        small = lax.psum_scatter(small, "ctx", scatter_dimension=0, axis_index_groups=groups)
    else:
        dw = dw[0]
        small = small[0]
    dw = lax.psum_scatter(dw, "fsdp", scatter_dimension=0).astype(F32).transpose(0, 2, 1)
    small = lax.psum_scatter(small, "fsdp", scatter_dimension=0)

    full = jnp.stack([gathered(w) for w in projections], 1)
    full = full.reshape(width, 4, HEAD_COUNT, HEAD_SIZE).transpose(0, 2, 1, 3).reshape(width, -1)
    grad_normed = nt(to_rows(d_pre).reshape(every, -1), full)
    scaled_first = grad_normed * norm_first
    gain_first = jnp.sum(grad_normed * inputs * first_scale, 0)
    grad_inputs = (
        first_scale * scaled_first
        - inputs * first_scale**3 * jnp.mean(scaled_first * inputs, -1, keepdims=True)
        + grad_middle
    )
    gains = jnp.stack([gain_first, gain_second], 0)
    gains = lax.psum_scatter(gains, both, scatter_dimension=1, tiled=True)
    conv_shard = small[: 3 * taps_count].reshape(3, taps_count, -1)
    return (
        result.reshape(tokens.shape),
        grad_inputs.astype(BF).reshape(tokens.shape),
        dw[0],
        dw[1],
        dw[2],
        dw[3],
        grad_output,
        grad_ffgate,
        grad_ffup,
        grad_ffdown,
        conv_shard,
        gains[0],
        gains[1],
        small[3 * taps_count],
    )


def solution(mesh):
    rows = P(None, "fsdp", "ctx", None)
    weight = P("fsdp", None)
    grad = P(None, ("ctx", "fsdp"))
    line = P(("ctx", "fsdp"))
    return jax.shard_map(
        body,
        mesh=mesh,
        in_specs=(rows, P(None, "fsdp"), *([weight] * 8), P(), P(), P(), P(), rows),
        out_specs=(rows, rows, *([grad] * 8), P(None, None, ("ctx", "fsdp")), line, line, line),
        check_vma=False,
    )
```

```python
from functools import partial

import jax
import jax.numpy as jnp
from jax import lax
from jax.experimental import pallas as pl
from jax.experimental.pallas import tpu as pltpu
from jax.sharding import PartitionSpec as P

HEAD_COUNT = 8
HEAD_SIZE = 128
C = 128
EPS = 1e-06
GROUP = 4
PAD = 8
BF = jnp.bfloat16
F32 = jnp.float32
VMEM_BYTES = 56 * 1024 * 1024


def nn(a, b):
    return lax.dot_general(a, b, (((1,), (0,)), ((), ())), preferred_element_type=F32)


def nt(a, b):
    return lax.dot_general(a, b, (((1,), (1,)), ((), ())), preferred_element_type=F32)


def tn(a, b):
    return lax.dot_general(a, b, (((0,), (0,)), ((), ())), preferred_element_type=F32)


def silu(v):
    return v * jax.nn.sigmoid(v)


def slope(v):
    s = jax.nn.sigmoid(v)
    return s * (1.0 + v * (1.0 - s))


def rowsum(v):
    return jnp.sum(v, -1, keepdims=True)


def place_of(step, count):
    per_half = count // GROUP
    pair = step // (2 * per_half)
    rest = step % (2 * per_half)
    first = rest < per_half
    group = jnp.where(first, rest, 2 * per_half - 1 - rest)
    return group, pair * 2 + jnp.where(first, 0, 1), first


def causal_mask():
    rows = lax.broadcasted_iota(jnp.int32, (C, C), 0)
    cols = lax.broadcasted_iota(jnp.int32, (C, C), 1)
    return rows >= cols


def valid_rows(step, length):
    pos = step * (GROUP * C) + lax.broadcasted_iota(jnp.int32, (GROUP * C, 1), 0)
    return (pos < length).astype(F32)


def split(v):
    high = v.astype(BF)
    return high, (v - high.astype(F32)).astype(BF)


def fine(product, a, b):
    (ah, al), (bh, bl) = a, b
    return product(ah, bh) + (product(ah, bl) + product(al, bh))


def each(f, *lists):
    return [f(*values) for values in zip(*lists)]


def masked(tri, values):
    return [jnp.where(tri, v, 0.0) for v in values]


def low(values):
    return [v.astype(BF) for v in values]


def beside(a, b):
    return jnp.concatenate([a, b], 1)


def solve(q, kb, skk, ridge, tri):
    system = each(lambda k, s: jnp.concatenate([k, s], 0), kb, skk)
    qb = low(q)
    inner0 = masked(tri, each(nt, qb, kb))
    i0 = each(lambda n, d, m, v: nn(beside(n, d), m) + ridge * v, low(inner0), qb, system, q)
    rr0 = each(lambda v: rowsum(v * v), q)
    p0 = each(lambda v, i: rowsum(v * i), q, i0)
    a0 = each(lambda r, p: r / p, rr0, p0)
    r1 = each(lambda v, a, i: v - a * i, q, a0, i0)
    f = each(lambda v: rowsum(v * v), r1)
    b = each(lambda v, r: v / r, f, rr0)
    d1 = each(lambda r, w, v: r + w * v, r1, b, q)
    db = low(d1)
    inner1 = masked(tri, each(nt, db, kb))
    i1 = each(lambda n, d, m, v: nn(beside(n, d), m) + ridge * v, low(inner1), db, system, d1)
    p1 = each(lambda v, i: rowsum(v * i), d1, i1)
    a1 = each(lambda v, p: v / p, f, p1)
    s2 = each(lambda a, v, w, d: a * v + w * d, a0, q, a1, d1)
    return system, qb, inner0, i0, rr0, p0, a0, r1, f, b, d1, db, inner1, i1, p1, a1, s2


def forward_kernel(
    count, len_ref, x_ref, w_ref, taps_ref, ridge_ref,
    gated_ref, pre_ref, mixed_ref, states_ref,
    padded, q_s, k_s, v_s, skk, skv,
):
    micro, step = pl.program_id(0), pl.program_id(1)
    _, _, first = place_of(step, count)
    span = GROUP * C

    @pl.when(step == 0)
    def _():
        padded[0:PAD, :] = jnp.zeros((PAD, 3 * HEAD_SIZE), F32)
        skk[...] = jnp.zeros_like(skk)
        skv[...] = jnp.zeros_like(skv)

    pre = nn(x_ref[...].reshape(span, x_ref.shape[-1]), w_ref[...])
    pre_ref[...] = pre.reshape(pre_ref.shape)
    for j in range(GROUP):
        jj = jnp.where(first, j, GROUP - 1 - j)
        padded[PAD + j * C : PAD + (j + 1) * C, :] = pre_ref[jj, 0, 0, :, : 3 * HEAD_SIZE]
    conv = taps_ref[0:1, :] * padded[PAD : PAD + span, :]
    for lag in range(1, 4):
        conv = conv + taps_ref[lag : lag + 1, :] * padded[PAD - lag : PAD - lag + span, :]
    padded[0:PAD, :] = padded[span : span + PAD, :]
    act = silu(conv)
    valid = valid_rows(step, len_ref[micro])
    act_q = act[:, :HEAD_SIZE]
    act_k = act[:, HEAD_SIZE : 2 * HEAD_SIZE]
    q_s[...] = act_q * lax.rsqrt(rowsum(act_q * act_q) + EPS)
    k_s[...] = act_k * (lax.rsqrt(rowsum(act_k * act_k) + EPS) * valid)
    v_s[...] = act[:, 2 * HEAD_SIZE :] * valid
    tri = causal_mask()
    ridge = ridge_ref[...]
    places = [jnp.where(first, j, GROUP - 1 - j) for j in range(GROUP)]
    rows = [slice(j * C, (j + 1) * C) for j in range(GROUP)]
    keys = [split(k_s[r, :]) for r in rows]
    values = [split(v_s[r, :]) for r in rows]
    kb = [k[0] for k in keys]
    kk_all, kv_all = [skk[...]], [skv[...]]
    for j in range(GROUP):
        kk_all.append(kk_all[j] + tn(kb[j], kb[j]))
        kv_all.append(kv_all[j] + fine(tn, keys[j], values[j]))
    skk[...] = kk_all[GROUP]
    skv[...] = kv_all[GROUP]
    for j, jj in enumerate(places):
        states_ref[jj, 0, 0, 0] = kk_all[j]
        states_ref[jj, 0, 0, 1] = kv_all[j]
    queries = [q_s[r, :] for r in rows]
    s2 = solve(queries, kb, low(kk_all[:GROUP]), ridge, tri)[-1]
    parts = [split(v) for v in s2]
    weights = [split(jnp.where(tri, fine(nt, a, k), 0.0)) for a, k in zip(parts, keys)]
    states = [split(v) for v in kv_all[:GROUP]]
    mixed = [
        (fine(nn, w, v) + fine(nn, a, t)) * valid[r, :]
        for w, v, a, t, r in zip(weights, values, parts, states, rows)
    ]
    for jj, v in zip(places, mixed):
        mixed_ref[jj, 0, 0] = v
        gate = pre_ref[jj, 0, 0, :, 3 * HEAD_SIZE :]
        gated_ref[jj, 0, 0] = (v * silu(gate)).astype(BF)


def attention_forward(lengths, x, w, taps, ridge):
    count, micros, slots = x.shape[:3]
    width = x.shape[-1]
    steps = count * slots // GROUP

    def at(m, s):
        group, slot, _ = place_of(s, count)
        return (group, m, slot, 0, 0)

    def at_state(m, s):
        group, slot, _ = place_of(s, count)
        return (group, m, slot, 0, 0, 0)

    def block(columns):
        return pl.BlockSpec((GROUP, 1, 1, C, columns), at)

    whole = lambda shape: pl.BlockSpec(shape, lambda m, s: (0,) * len(shape))
    lead = (count, micros, slots, C)
    return pl.pallas_call(
        partial(forward_kernel, count),
        grid=(micros, steps),
        in_specs=[
            pl.BlockSpec(memory_space=pltpu.SMEM),
            block(width),
            whole(w.shape),
            whole(taps.shape),
            whole(ridge.shape),
        ],
        out_specs=[
            block(HEAD_SIZE),
            block(4 * HEAD_SIZE),
            block(HEAD_SIZE),
            pl.BlockSpec((GROUP, 1, 1, 2, HEAD_SIZE, HEAD_SIZE), at_state),
        ],
        out_shape=[
            jax.ShapeDtypeStruct((*lead, HEAD_SIZE), BF),
            jax.ShapeDtypeStruct((*lead, 4 * HEAD_SIZE), F32),
            jax.ShapeDtypeStruct((*lead, HEAD_SIZE), F32),
            jax.ShapeDtypeStruct((count, micros, slots, 2, HEAD_SIZE, HEAD_SIZE), F32),
        ],
        scratch_shapes=[
            pltpu.VMEM((GROUP * C + PAD, 3 * HEAD_SIZE), F32),
            pltpu.VMEM((GROUP * C, HEAD_SIZE), F32),
            pltpu.VMEM((GROUP * C, HEAD_SIZE), F32),
            pltpu.VMEM((GROUP * C, HEAD_SIZE), F32),
            pltpu.VMEM((HEAD_SIZE, HEAD_SIZE), F32),
            pltpu.VMEM((HEAD_SIZE, HEAD_SIZE), F32),
        ],
        compiler_params=pltpu.CompilerParams(vmem_limit_bytes=VMEM_BYTES),
        cost_estimate=pl.CostEstimate(
            flops=2 * count * micros * slots * C * (width * 512 + 11 * C * C),
            bytes_accessed=count * micros * slots * C * (2 * width + 4096),
            transcendentals=0,
        ),
        name="attn_forward",
    )(lengths, x, w, taps, ridge)


def backward_kernel(
    count, steps, len_ref, x_ref, g_ref, pre_ref, tail_ref, mixed_ref, states_ref, taps_ref, ridge_ref,
    dpre_ref, dw_ref, dtaps_ref, dridge_ref,
    padded, conv_s, act_s, q_s, k_s, dq_s, dk_s, dv_s, ext, gsum, hsum,
):
    micro, turn = pl.program_id(0), pl.program_id(1)
    step = steps - 1 - turn
    _, _, first = place_of(step, count)
    span = GROUP * C

    @pl.when(turn == 0)
    def _():
        ext[span : span + PAD, :] = jnp.zeros((PAD, 3 * HEAD_SIZE), F32)
        gsum[...] = jnp.zeros_like(gsum)
        hsum[...] = jnp.zeros_like(hsum)

    @pl.when((turn == 0) & (micro == 0))
    def _():
        dw_ref[...] = jnp.zeros_like(dw_ref)
        dtaps_ref[...] = jnp.zeros_like(dtaps_ref)
        dridge_ref[...] = jnp.zeros_like(dridge_ref)

    keep = jnp.where(step > 0, 1.0, 0.0)
    padded[0:PAD, :] = tail_ref[0, 0, 0, :, : 3 * HEAD_SIZE] * keep
    for j in range(GROUP):
        jj = jnp.where(first, j, GROUP - 1 - j)
        padded[PAD + j * C : PAD + (j + 1) * C, :] = pre_ref[jj, 0, 0, :, : 3 * HEAD_SIZE]
    conv = taps_ref[0:1, :] * padded[PAD : PAD + span, :]
    for lag in range(1, 4):
        conv = conv + taps_ref[lag : lag + 1, :] * padded[PAD - lag : PAD - lag + span, :]
    conv_s[...] = conv
    act = silu(conv)
    act_s[...] = act
    valid = valid_rows(step, len_ref[micro])
    act_q = act[:, :HEAD_SIZE]
    act_k = act[:, HEAD_SIZE : 2 * HEAD_SIZE]
    scale_q = lax.rsqrt(rowsum(act_q * act_q) + EPS)
    scale_k = lax.rsqrt(rowsum(act_k * act_k) + EPS)
    q_s[...] = act_q * scale_q
    k_s[...] = act_k * (scale_k * valid)
    tri = causal_mask()
    ridge = ridge_ref[...]
    places = [jnp.where(first, j, GROUP - 1 - j) for j in range(GROUP)]
    rows = [slice(j * C, (j + 1) * C) for j in range(GROUP)]
    q = [q_s[r, :] for r in rows]
    keys = [split(k_s[r, :]) for r in rows]
    kb = [k[0] for k in keys]
    values = [split(act_s[r, 2 * HEAD_SIZE :] * valid[r, :]) for r in rows]
    vb = [v[0] for v in values]
    skk = [states_ref[jj, 0, 0, 0].astype(BF) for jj in places]
    skv = [split(states_ref[jj, 0, 0, 1]) for jj in places]
    g = []
    for jj, r in zip(places, rows):
        gate = pre_ref[jj, 0, 0, :, 3 * HEAD_SIZE :]
        d_gated = g_ref[jj, 0, 0].astype(F32)
        dpre_ref[jj, 0, 0, :, 3 * HEAD_SIZE :] = (
            d_gated * mixed_ref[jj, 0, 0] * slope(gate)
        ).astype(BF)
        g.append(split(d_gated * silu(gate) * valid[r, :]))
    gb = [v[0] for v in g]
    system, qb, inner0, i0, rr0, p0, a0, r1, f, b, d1, d1b, inner1, i1, p1, a1, s2 = solve(
        q, kb, skk, ridge, tri
    )
    back = masked(tri, [fine(nt, v, w) for v, w in zip(g, values)])
    ds = [
        fine(nn, split(w), k) + fine(nt, v, t) for w, k, v, t in zip(back, keys, g, skv)
    ]
    sb = low(s2)
    p = low(masked(tri, each(nt, sb, kb)))
    da1 = each(lambda v, d: rowsum(v * d), ds, d1)
    df = each(lambda v, w: v / w, da1, p1)
    dp1 = each(lambda v, a: -v * a, df, a1)
    dd1 = each(lambda a, v, w, i: a * v + (2.0 * w) * i, a1, ds, dp1, i1)
    dbeta = each(lambda v, w: rowsum(v * w), dd1, q)
    inv_rr = each(lambda v: 1.0 / v, rr0)
    df = each(lambda v, w, i: v + w * i, df, dbeta, inv_rr)
    dr1 = each(lambda v, w, r: v + (2.0 * w) * r, dd1, df, r1)
    drb = low(dr1)
    innerr = masked(tri, each(nt, drb, kb))
    adr = each(lambda n, d, m, v: nn(beside(n, d), m) + ridge * v, low(innerr), drb, system, dr1)
    da0p = each(lambda v, w, r, i, z: rowsum(v * w - r * i) / z, ds, q, dr1, i0, p0)
    drr = each(lambda v, w, i, z: z - v * w * i, dbeta, b, inv_rr, da0p)
    dp0 = each(lambda v, a: -v * a, da0p, a0)
    dd0 = each(
        lambda w, v, a, t, e, i, m: w * v + a * t + (2.0 * e) * i - a * m,
        b, dd1, a0, ds, dp0, i0, adr,
    )
    di0 = each(lambda e, v, a, r: e * v - a * r, dp0, q, a0, dr1)
    for r, v, w, z, t in zip(rows, dr1, dd0, drr, q):
        dq_s[r, :] = v + w + (2.0 * z) * t
    wd1 = each(lambda e, d: (2.0 * e) * d, dp1, d1)
    inneri = low(each(lambda e, n, a, m: e * n - a * m, dp0, inner0, a0, innerr))
    di0b = low(di0)
    wd1b = low(wd1)
    ridge_total = sum(
        jnp.sum(0.5 * w * d + e * v, 0, keepdims=True) for w, d, e, v in zip(wd1, d1, di0, q)
    )
    left = each(
        lambda *parts: jnp.concatenate(parts, 0), low(back), low(inner1), low(inner0), inneri
    )
    right = each(lambda *parts: jnp.concatenate(parts, 0), sb, wd1b, di0b, qb)
    near = each(tn, left, right)
    both = each(lambda w, v, t: tn(beside(w, v), t), p, sb, gb)
    outer = each(
        lambda d, e, v, w: tn(jnp.concatenate([d, e, v], 0), jnp.concatenate([w, v, e], 0)),
        d1b, di0b, qb, wd1b,
    )
    g_all, h_all = [gsum[...]], [hsum[...]]
    for j in reversed(range(GROUP)):
        g_all.insert(0, g_all[0] + outer[j])
        h_all.insert(0, h_all[0] + both[j][C:])
    gsum[...] = g_all[0]
    hsum[...] = h_all[0]
    for j, r in enumerate(rows):
        hb = h_all[j + 1].astype(BF)
        dk_s[r, :] = near[j] + nn(kb[j], g_all[j + 1].astype(BF)) + nt(vb[j], hb)
        dv_s[r, :] = both[j][:C] + nn(kb[j], hb)
    dridge_ref[...] += ridge_total
    act = act_s[...]
    act_q = act[:, :HEAD_SIZE]
    act_k = act[:, HEAD_SIZE : 2 * HEAD_SIZE]
    dq = dq_s[...]
    dk = dk_s[...] * valid
    d_act_q = scale_q * dq - act_q * (scale_q * scale_q * scale_q * rowsum(dq * act_q))
    d_act_k = scale_k * dk - act_k * (scale_k * scale_k * scale_k * rowsum(dk * act_k))
    d_act = jnp.concatenate([d_act_q, d_act_k, dv_s[...] * valid], 1)
    ext[0:span, :] = d_act * slope(conv_s[...])
    now = padded[PAD : PAD + span, :]
    shifted = ext[0:span, :]
    d_pre = taps_ref[0:1, :] * shifted
    dtaps_ref[0:1, :] += jnp.sum(shifted * now, 0, keepdims=True)
    for lag in range(1, 4):
        shifted = ext[lag : lag + span, :]
        d_pre = d_pre + taps_ref[lag : lag + 1, :] * shifted
        dtaps_ref[lag : lag + 1, :] += jnp.sum(shifted * now, 0, keepdims=True)
    ext[span : span + PAD, :] = ext[0:PAD, :]
    d_pre = d_pre.astype(BF)
    for j in range(GROUP):
        jj = jnp.where(first, j, GROUP - 1 - j)
        dpre_ref[jj, 0, 0, :, : 3 * HEAD_SIZE] = d_pre[j * C : (j + 1) * C, :]
    dw_ref[...] += tn(
        dpre_ref[...].reshape(span, 4 * HEAD_SIZE), x_ref[...].reshape(span, x_ref.shape[-1])
    )


def attention_backward(lengths, x, d_gated, pre, mixed, states, taps, ridge):
    count, micros, slots = x.shape[:3]
    width = x.shape[-1]
    steps = count * slots // GROUP

    def at(m, s):
        group, slot, _ = place_of(steps - 1 - s, count)
        return (group, m, slot, 0, 0)

    def at_state(m, s):
        group, slot, _ = place_of(steps - 1 - s, count)
        return (group, m, slot, 0, 0, 0)

    def at_tail(m, s):
        step = jnp.maximum(steps - 2 - s, 0)
        group, slot, first = place_of(step, count)
        device = group * GROUP + jnp.where(first, GROUP - 1, 0)
        return (device, m, slot, C // PAD - 1, 0)

    def block(columns):
        return pl.BlockSpec((GROUP, 1, 1, C, columns), at)

    whole = lambda shape: pl.BlockSpec(shape, lambda m, s: (0,) * len(shape))
    rows = GROUP * C
    return pl.pallas_call(
        partial(backward_kernel, count, steps),
        grid=(micros, steps),
        in_specs=[
            pl.BlockSpec(memory_space=pltpu.SMEM),
            block(width),
            block(HEAD_SIZE),
            block(4 * HEAD_SIZE),
            pl.BlockSpec((1, 1, 1, PAD, 4 * HEAD_SIZE), at_tail),
            block(HEAD_SIZE),
            pl.BlockSpec((GROUP, 1, 1, 2, HEAD_SIZE, HEAD_SIZE), at_state),
            whole(taps.shape),
            whole(ridge.shape),
        ],
        out_specs=[
            block(4 * HEAD_SIZE),
            whole((4 * HEAD_SIZE, width)),
            whole((PAD, 3 * HEAD_SIZE)),
            whole((1, HEAD_SIZE)),
        ],
        out_shape=[
            jax.ShapeDtypeStruct((count, micros, slots, C, 4 * HEAD_SIZE), BF),
            jax.ShapeDtypeStruct((4 * HEAD_SIZE, width), F32),
            jax.ShapeDtypeStruct((PAD, 3 * HEAD_SIZE), F32),
            jax.ShapeDtypeStruct((1, HEAD_SIZE), F32),
        ],
        scratch_shapes=[
            pltpu.VMEM((rows + PAD, 3 * HEAD_SIZE), F32),
            pltpu.VMEM((rows, 3 * HEAD_SIZE), F32),
            pltpu.VMEM((rows, 3 * HEAD_SIZE), F32),
            pltpu.VMEM((rows, HEAD_SIZE), F32),
            pltpu.VMEM((rows, HEAD_SIZE), F32),
            pltpu.VMEM((rows, HEAD_SIZE), F32),
            pltpu.VMEM((rows, HEAD_SIZE), F32),
            pltpu.VMEM((rows, HEAD_SIZE), F32),
            pltpu.VMEM((rows + PAD, 3 * HEAD_SIZE), F32),
            pltpu.VMEM((HEAD_SIZE, HEAD_SIZE), F32),
            pltpu.VMEM((HEAD_SIZE, HEAD_SIZE), F32),
        ],
        compiler_params=pltpu.CompilerParams(vmem_limit_bytes=VMEM_BYTES),
        cost_estimate=pl.CostEstimate(
            flops=2 * count * micros * slots * C * (width * 512 + 24 * C * C),
            bytes_accessed=count * micros * slots * C * (2 * width + 4096),
            transcendentals=0,
        ),
        name="attn_backward",
    )(lengths, x, d_gated, pre, pre, mixed, states, taps, ridge)


def ff_kernel(
    x_ref, up_ref, mid_ref, xs_ref, us_ref, wg_ref, wu_ref, wd_ref,
    res_ref, d2_ref, gk_ref, gs_ref, uk_ref, us_out_ref, dk_ref, ds_ref, total,
):
    tile = pl.program_id(0)
    last = pl.num_programs(0) - 1
    half = xs_ref.shape[1] // 2

    @pl.when(tile == 0)
    def _():
        total[...] = mid_ref[...]
        d2_ref[...] = jnp.zeros_like(d2_ref)

    x = x_ref[...]
    swish_pre = nn(x, wg_ref[...])
    lift = nn(x, wu_ref[...])
    sig = jax.nn.sigmoid(swish_pre)
    swish = swish_pre * sig
    hidden = (swish * lift).astype(BF)
    total[...] += nn(hidden, wd_ref[...])
    d_hidden = nt(up_ref[...], wd_ref[...])
    d_swish = (d_hidden * lift * (sig * (1.0 + swish_pre * (1.0 - sig)))).astype(BF)
    d_lift = (d_hidden * swish).astype(BF)
    d2_ref[...] += nt(d_swish, wg_ref[...]) + nt(d_lift, wu_ref[...])
    xs = xs_ref[...]
    gate = tn(d_swish, xs).astype(BF)
    gk_ref[...] = gate[:, :half]
    gs_ref[...] = gate[:, half:]
    lifted = tn(d_lift, xs).astype(BF)
    uk_ref[...] = lifted[:, :half]
    us_out_ref[...] = lifted[:, half:]
    down = tn(us_ref[...], hidden).astype(BF)
    dk_ref[...] = down[:half]
    ds_ref[...] = down[half:]

    @pl.when(tile == last)
    def _():
        res_ref[...] = total[...].astype(BF)


def feed_forward(x, up, middle, x_split, up_split, wg, wu, wd):
    rows, width = x.shape
    ff = wg.shape[1]
    tile = 256
    half = width // 2
    whole = pl.BlockSpec((rows, width), lambda t: (0, 0))
    across = pl.BlockSpec((width, tile), lambda t: (0, t))
    down = pl.BlockSpec((tile, width), lambda t: (t, 0))
    tall = pl.BlockSpec((tile, half), lambda t: (t, 0))
    wide = pl.BlockSpec((half, tile), lambda t: (0, t))
    tall_shape = jax.ShapeDtypeStruct((ff, half), BF)
    wide_shape = jax.ShapeDtypeStruct((half, ff), BF)
    return pl.pallas_call(
        ff_kernel,
        grid=(ff // tile,),
        in_specs=[whole, whole, whole, whole, whole, across, across, down],
        out_specs=[whole, whole, tall, tall, tall, tall, wide, wide],
        out_shape=[
            jax.ShapeDtypeStruct((rows, width), BF),
            jax.ShapeDtypeStruct((rows, width), F32),
            *([tall_shape] * 4),
            *([wide_shape] * 2),
        ],
        scratch_shapes=[pltpu.VMEM((rows, width), F32)],
        compiler_params=pltpu.CompilerParams(vmem_limit_bytes=VMEM_BYTES),
        cost_estimate=pl.CostEstimate(
            flops=18 * rows * width * ff, bytes_accessed=12 * width * ff, transcendentals=rows * ff
        ),
        name="feed_forward",
    )(x, up, middle, x_split, up_split, wg, wu, wd)


def input_kernel(
    d_ref, w_ref, in_ref, mid_ref, gain_ref, out_ref, total,
):
    head = pl.program_id(0)

    @pl.when(head == 0)
    def _():
        total[...] = jnp.zeros_like(total)

    total[...] += nt(d_ref[0], w_ref[0])

    @pl.when(head == pl.num_programs(0) - 1)
    def _():
        inputs = in_ref[...].astype(F32)
        scale = lax.rsqrt(jnp.mean(inputs * inputs, -1, keepdims=True) + EPS)
        grad = total[...]
        scaled = grad * gain_ref[...]
        mean = jnp.mean(scaled * inputs, -1, keepdims=True)
        out_ref[...] = (
            scale * scaled - inputs * (scale * scale * scale * mean) + mid_ref[...]
        ).astype(BF)


def input_gradient(d_pre, weights, tokens, grad_middle, gain):
    heads, rows, columns = d_pre.shape
    width = tokens.shape[1]
    whole = lambda shape: pl.BlockSpec(shape, lambda h: (0,) * len(shape))
    return pl.pallas_call(
        input_kernel,
        grid=(heads,),
        in_specs=[
            pl.BlockSpec((1, rows, columns), lambda h: (h, 0, 0)),
            pl.BlockSpec((1, width, columns), lambda h: (h, 0, 0)),
            whole((rows, width)),
            whole((rows, width)),
            whole((1, width)),
        ],
        out_specs=whole((rows, width)),
        out_shape=jax.ShapeDtypeStruct((rows, width), BF),
        scratch_shapes=[pltpu.VMEM((rows, width), F32)],
        compiler_params=pltpu.CompilerParams(vmem_limit_bytes=VMEM_BYTES),
        cost_estimate=pl.CostEstimate(
            flops=2 * rows * heads * columns * width,
            bytes_accessed=2 * heads * columns * (rows + width),
            transcendentals=0,
        ),
        name="input_gradient",
    )(d_pre, weights, tokens, grad_middle, gain)


def owner_bits(skip):
    sizes = {axis: lax.axis_size(axis) for axis in ("ctx", "fsdp")}
    bits = [
        (axis, 1 << i)
        for axis in ("ctx", "fsdp")
        for i in reversed(range(sizes[axis].bit_length() - 1))
    ]
    return bits[: len(bits) - skip]


def swapped(value, axis, bit):
    return lax.ppermute(value, axis, [(i, i ^ bit) for i in range(lax.axis_size(axis))])


class Halving:
    def __init__(self, value, bits, order):
        self.left = list(bits)
        self.order = order + [b for b in reversed(bits) if b not in order]
        self.dtype = value.dtype
        rows = value.shape[0] >> len(bits)
        self.value = value.reshape(*([2] * len(bits)), rows, *value.shape[1:])

    def start(self):
        axis, bit = self.order[0]
        dim = self.left.index(self.order[0])
        mine = lax.axis_index(axis) // bit % 2
        self.keep = lax.dynamic_index_in_dim(self.value, mine, dim, False)
        self.send = lax.dynamic_index_in_dim(self.value, 1 - mine, dim, False)

    def finish(self):
        axis, bit = self.order.pop(0)
        self.left.remove((axis, bit))
        got = swapped(self.send, axis, bit)
        self.value = (self.keep.astype(F32) + got.astype(F32)).astype(self.dtype)

    def result(self):
        while self.order:
            self.start()
            self.finish()
        return self.value


def around(value, axis, stride):
    size = lax.axis_size(axis)
    place = lax.axis_index(axis)
    ring = [(i, (i + stride) % size) for i in range(size)]
    across = [(i, i ^ 1) for i in range(size)]
    every = jnp.zeros((size, *value.shape), value.dtype)
    for hop in range(size // stride):
        source = lax.rem(place - hop * stride + size, size)
        every = lax.dynamic_update_index_in_dim(every, value, source, 0)
        other = lax.ppermute(value, axis, across)
        if hop + 1 < size // stride:
            value = lax.ppermute(value, axis, ring)
        every = lax.dynamic_update_index_in_dim(every, other, source ^ 1, 0)
    return every


def body(
    tokens,
    lengths,
    w_query,
    w_key,
    w_value,
    w_mixgate,
    w_output,
    w_ffgate,
    w_ffup,
    w_ffdown,
    conv_weight,
    norm_first,
    norm_second,
    ridge_log,
    out_grad,
):
    micros, _, rows, width = tokens.shape
    taps_count = conv_weight.shape[1]
    count = lax.axis_size("ctx")
    shards = lax.axis_size("fsdp")
    place = lax.axis_index("ctx")
    share = count // HEAD_COUNT
    own = max(micros // share, 1)
    copies = share * own // micros
    head = place // share
    column = head * HEAD_SIZE
    slots = rows // C
    every = micros * rows

    def gathered(w):
        return lax.all_gather(w, "fsdp", axis=0, tiled=True)

    def of_head(w, axis):
        return lax.dynamic_slice_in_dim(w, column, HEAD_SIZE, axis)

    projections = (w_query, w_key, w_value, w_mixgate)
    w_head = gathered(jnp.concatenate([of_head(w, 1) for w in projections], 1))
    taps = of_head(conv_weight, 2).transpose(1, 0, 2).reshape(taps_count, 3 * HEAD_SIZE)
    ridge = jnp.exp(of_head(ridge_log, 0))[None]
    full_output = gathered(w_output)
    full_ffgate = gathered(w_ffgate)
    full_ffup = gathered(w_ffup)
    full_ffdown = gathered(w_ffdown)
    inputs = tokens.reshape(micros, rows, width).astype(F32)
    first_scale = lax.rsqrt(jnp.mean(inputs * inputs, -1, keepdims=True) + EPS)
    normed = (inputs * first_scale * norm_first).astype(BF)
    mine = lax.rem(place, share) // copies * own
    own_lengths = lax.dynamic_slice_in_dim(lengths[:, 0], mine, own, 0)

    def to_rows(value):
        columns = value.shape[-1]
        value = value.reshape(count, -1, rows, columns)
        value = lax.all_to_all(value, "ctx", 0, 0)
        value = value.reshape(HEAD_COUNT, share // copies, copies, -1, columns)[:, :, 0]
        return value.reshape(HEAD_COUNT, -1, columns)

    def to_heads(value):
        value = value.reshape(share // copies, -1, rows, HEAD_COUNT, HEAD_SIZE)
        value = value.transpose(3, 0, 1, 2, 4)[:, :, None]
        value = jnp.broadcast_to(value, (*value.shape[:2], copies, *value.shape[3:]))
        value = value.reshape(count, -1, rows, HEAD_SIZE)
        value = lax.all_to_all(value, "ctx", 0, 0)
        return value.reshape(count, -1, slots, C, HEAD_SIZE)

    lanes = micros if share == 1 else 1
    states = []
    middles = []
    gateds = []
    for lane in range(lanes):
        part = normed[lane : lane + 1] if lanes > 1 else normed
        x = around(part, "ctx", 2)
        if share > 1:
            x = lax.dynamic_slice_in_dim(x, mine, own, 1)
        x = x.reshape(count, -1, slots, C, width)
        lane_lengths = own_lengths[lane : lane + 1] if lanes > 1 else own_lengths
        gated_head, pre, mixed, prefix = attention_forward(lane_lengths, x, w_head, taps, ridge)
        states.append((lane_lengths, x, pre, mixed, prefix))
        gated = to_rows(gated_head).transpose(1, 0, 2).reshape(-1, width)
        before = inputs[lane] if lanes > 1 else inputs.reshape(every, width)
        gateds.append(gated)
        middles.append(before + nn(gated, full_output))
    gated = jnp.concatenate(gateds, 0)
    middle = jnp.concatenate(middles, 0)
    second_scale = lax.rsqrt(jnp.mean(middle * middle, -1, keepdims=True) + EPS)
    normed_two = (middle * second_scale * norm_second).astype(BF)
    upstream = out_grad.reshape(every, width)
    core = lax.axis_index("fsdp") % 2
    devices = count * shards
    half = width // 2

    def halves(value):
        return [lax.dynamic_slice_in_dim(value, c * half, half, 1) for c in (core, 1 - core)]

    owned = upstream.reshape(every, devices // 2, 2, width // devices)
    up_split = jnp.concatenate(
        [
            lax.dynamic_index_in_dim(owned, c, 2, False).reshape(every, half)
            for c in (core, 1 - core)
        ],
        1,
    )
    x_split = jnp.concatenate(halves(normed_two), 1)
    result, grad_two, gate_keep, gate_send, up_keep, up_send, down_keep, down_send = feed_forward(
        normed_two, upstream, middle, x_split, up_split, full_ffgate, full_ffup, full_ffdown
    )

    def joined(keep, send, order):
        got = swapped(send, "fsdp", 1)
        value = (keep.astype(F32) + got.astype(F32)).astype(BF)
        return Halving(value, owner_bits(1), order)

    row, side = ("fsdp", 2), ("ctx", 1)
    sums = [
        joined(gate_keep, gate_send, [row, side]),
        joined(up_keep, up_send, [side, row]),
        joined(down_keep, down_send, [row, side]),
    ]
    scaled_two = grad_two * norm_second
    gain_second = jnp.sum(grad_two * middle * second_scale, 0)
    grad_middle = (
        second_scale * scaled_two
        - middle * second_scale**3 * jnp.mean(scaled_two * middle, -1, keepdims=True)
        + upstream.astype(F32)
    )
    grad_branch = grad_middle.astype(BF)
    gated_keep, gated_send = halves(gated)
    sums.append(
        joined(
            tn(grad_branch, gated_keep).astype(BF), tn(grad_branch, gated_send).astype(BF), [side, row]
        )
    )
    late = lax.optimization_barrier((gated, *projections))[1:]
    late = jnp.stack([w.reshape(-1, HEAD_COUNT, HEAD_SIZE) for w in late], 2)
    late = late.transpose(1, 0, 2, 3).reshape(HEAD_COUNT, -1, 4 * HEAD_SIZE)
    full = lax.all_gather(late, "fsdp", axis=1, tiled=True)
    span = every // lanes
    pieces = []
    d_rows = []
    for lane in range(lanes):
        at = slice(lane * span, (lane + 1) * span)
        grad_gated = nt(grad_branch[at], full_output).astype(BF)
        lane_lengths, x, pre, mixed, prefix = states[lane]
        grad_heads = to_heads(grad_gated)
        if lane == 0:
            for part in sums:
                part.start()
            tied = lax.optimization_barrier((grad_heads, *[part.send for part in sums]))
            grad_heads = tied[0]
            for part, send in zip(sums, tied[1:]):
                part.send = send
                part.finish()
        d_pre, dw, dtaps, dridge = attention_backward(
            lane_lengths, x, grad_heads, pre, mixed, prefix, taps, ridge
        )
        pieces.append((dw, dtaps, dridge))
        d_rows.append(to_rows(d_pre))
    dw, dtaps, dridge = (sum(values) for values in zip(*pieces))
    if copies > 1:
        counts = lax.rem(place, copies) == 0
        dw, dtaps, dridge = (jnp.where(counts, v, 0.0) for v in (dw, dtaps, dridge))
    gain_first = jnp.sum(w_head.astype(F32).T * dw, 0) / norm_first
    piece = HEAD_SIZE // share // shards
    dw = dw.reshape(4, share, shards, piece, width).transpose(1, 2, 0, 3, 4).astype(BF)
    if share > 1:
        groups = [[h * share + i for i in range(share)] for h in range(HEAD_COUNT)]
        dw = lax.psum_scatter(dw, "ctx", scatter_dimension=0, axis_index_groups=groups)
    else:
        dw = dw[0]
    dw = lax.psum_scatter(dw, "fsdp", scatter_dimension=0).astype(F32).transpose(0, 2, 1)
    dtaps = dtaps[:taps_count].reshape(taps_count, 3, HEAD_SIZE).transpose(1, 0, 2)
    small = jnp.concatenate([dtaps.reshape(3 * taps_count, HEAD_SIZE), dridge * ridge], 0)
    small = lax.dynamic_update_slice_in_dim(
        jnp.zeros((small.shape[0], width), F32), small, column, 1
    )
    small = jnp.concatenate([small, gain_first[None], gain_second[None]], 0)
    small = small.reshape(-1, devices, width // devices).transpose(1, 0, 2)
    small = Halving(small, owner_bits(0), []).result()[0]

    def columns_of(part):
        rows_now = part.result()
        rows_now = rows_now.reshape(2, -1, half)
        keep = lax.dynamic_index_in_dim(rows_now, core, 0, False)
        got = swapped(lax.dynamic_index_in_dim(rows_now, 1 - core, 0, False), "fsdp", 1)
        pair = jnp.where(core == 0, jnp.stack([keep, got]), jnp.stack([got, keep]))
        return pair.astype(F32).transpose(0, 2, 1).reshape(width, -1)

    grad_ffgate, grad_ffup, grad_output = (columns_of(sums[i]) for i in (0, 1, 3))
    grad_ffdown = sums[2].result().astype(F32).T

    out_rows = []
    for lane in range(lanes):
        at = slice(lane * span, (lane + 1) * span)
        grad_inputs = input_gradient(
            d_rows[lane], full, tokens.reshape(every, width)[at], grad_middle[at], norm_first[None]
        )
        out_rows.append(grad_inputs)
    conv_shard = small[: 3 * taps_count].reshape(3, taps_count, -1)
    return (
        result.reshape(tokens.shape),
        jnp.concatenate(out_rows, 0).reshape(tokens.shape),
        dw[0],
        dw[1],
        dw[2],
        dw[3],
        grad_output,
        grad_ffgate,
        grad_ffup,
        grad_ffdown,
        conv_shard,
        small[3 * taps_count + 1],
        small[3 * taps_count + 2],
        small[3 * taps_count],
    )


def solution(mesh):
    rows = P(None, "fsdp", "ctx", None)
    weight = P("fsdp", None)
    grad = P(None, ("ctx", "fsdp"))
    line = P(("ctx", "fsdp"))
    return jax.shard_map(
        body,
        mesh=mesh,
        in_specs=(rows, P(None, "fsdp"), *([weight] * 8), P(), P(), P(), P(), rows),
        out_specs=(rows, rows, *([grad] * 8), P(None, None, ("ctx", "fsdp")), line, line, line),
        check_vma=False,
    )
```
